32 devices in a mesh: groups: 2 (over x), blk: 4 (over y, core), row: 4 (over z).
Axes of the slice: x: 2, y: 2, z: 4, core: 2. Of those that a mesh axis runs over, the one named last changes fastest.
Arguments:
- coords: float32 [3, 24576], P(None, ('groups', 'blk', 'row')), parts along dimension 1, may hold values from 0 to 1
- charges: float32 [24576], P(('groups', 'blk', 'row')), parts along dimension 0, may hold values from -1 to 1
- counts: int32 [32], P(('groups', 'blk', 'row')), parts along dimension 0, may hold values from 256 to 768, as said below
- send_slot: int32 [24576], P(('groups', 'blk', 'row')), parts along dimension 0, may hold values from 0 to 1023, as said below
- recv_index: int32 [16384], P(('groups', 'blk', 'row')), parts along dimension 0, may hold values from 0 to 1023, as said below
- wave_ints: int32 [3, 24576], P(None, 'blk'), may hold values from -36 to 36, as said below
Outputs:
- slot_forces: float32 [3, 24576], P(None, ('groups', 'blk', 'row')), parts along dimension 1
- atom_forces: float32 [3, 16384], P(None, ('groups', 'blk', 'row')), parts along dimension 1
The draws below stay inside these ranges and needn't reach their ends.
There are 2 independent parts, one for each index of `groups`. The reference program is written for one: setup_inputs(seed, part) draws one part's arguments, and reference() takes and returns one part's arrays. A program takes and returns all parts, laid end to end along the dimension named above; an argument that names none is the same for every part. Nothing has to cross between parts.
Inputs may be any that keep to these rules, and one draw needn't show every extreme that they name: The counts of one system sum to 8192; the largest is 768. `send_slot`: for a live slot the value is d * 64 + r: the ion goes to k-space device d as its r-th arrival from this owner. Live values of one owner are distinct, and the ranks r to one device are 0 up to the number sent there minus one. Every device receives exactly 512 ions; some owner sends exactly 64 to some device. Slots that are not live hold arbitrary values. `recv_index`: the 512 values of device d are distinct and are exactly the arrivals s * 64 + r sent to d. `wave_ints`: each column is (h, k, l) with |h|, |k| at most 12 and l nonzero.
All inputs are finite; a program needn't handle non-finite values.
Results may differ from the reference program's by a relative error of at most 0.00007.
Values sent between devices are 32-bit elements; how exact they have to be, the bound alone decides.
A program may use at most 128 MiB of HBM per device.

```python
import math
import jax
import jax.numpy as jnp
from jax import lax

A_DEV = 512
K = 24576
HMAX = 12
LMAX = 36
PEERS = 16
SLOTS_DEV = 768
ION_SLOT_TOTAL = 12288
PAIR_CAP = 64


def balanced_loads(sub_key, half_load):
    pair_count = PEERS // 2
    key_swing, key_order = jax.random.split(sub_key)
    swing = jax.random.randint(key_swing, (pair_count,), -half_load, half_load + 1)
    swing = swing.at[0].set(half_load)
    loads = jnp.stack([half_load + swing, half_load - swing], axis=1).reshape(-1)
    order = jax.random.permutation(key_order, PEERS)
    return loads[order].astype(jnp.int32)


def routing_tables(key):
    base = jax.random.fold_in(key, 7)
    keys = jax.random.split(base, 5)
    half_load = A_DEV // (2 * PEERS)
    owner_load = balanced_loads(keys[0], half_load)
    shared_load = balanced_loads(keys[1], half_load)
    peer_ids = jnp.arange(PEERS, dtype=jnp.int32)
    shifted = (peer_ids[:, None] + peer_ids[None, :]) % PEERS
    sent = owner_load[:, None] + shared_load[shifted]
    counts = jnp.sum(sent, axis=1).astype(jnp.int32)
    flat_ids = jnp.arange(PEERS * PAIR_CAP, dtype=jnp.int32)
    ranks = flat_ids % PAIR_CAP
    partner = flat_ids // PAIR_CAP

    def owner_slots(sub_key, owner):
        usable = ranks < sent[owner, partner]
        scores = jnp.where(usable, jax.random.permutation(sub_key, PEERS * PAIR_CAP).astype(jnp.int32), PEERS * PAIR_CAP + flat_ids)
        return jnp.argsort(scores, stable=True)[:SLOTS_DEV].astype(jnp.int32)
    send_keys = jax.random.split(keys[2], PEERS)
    outbound_rows = jax.vmap(owner_slots)(send_keys, peer_ids)
    slot_ids = jnp.arange(SLOTS_DEV, dtype=jnp.int32)
    filler = jax.random.randint(keys[3], (PEERS, SLOTS_DEV), 0, PEERS * PAIR_CAP)
    send_slot = jnp.where(slot_ids[None, :] < counts[:, None], outbound_rows, filler).reshape(-1).astype(jnp.int32)

    def device_rows(sub_key, device):
        usable = ranks < sent[partner, device]
        scores = jnp.where(usable, jax.random.permutation(sub_key, PEERS * PAIR_CAP).astype(jnp.int32), PEERS * PAIR_CAP + flat_ids)
        return jnp.argsort(scores, stable=True)[:A_DEV].astype(jnp.int32)
    recv_keys = jax.random.split(keys[4], PEERS)
    recv_index = jax.vmap(device_rows)(recv_keys, peer_ids).reshape(-1).astype(jnp.int32)
    return (counts, send_slot, recv_index)


def draw_counts(key, part):
    return routing_tables(key)[0]


def draw_send_slot(key, part):
    return routing_tables(key)[1]


def draw_recv_index(key, part):
    return routing_tables(key)[2]


def draw_wave_ints(key, part):
    keys = jax.random.split(jax.random.fold_in(key, 11), 4)
    first = jax.random.randint(keys[0], (K,), -HMAX, HMAX + 1)
    second = jax.random.randint(keys[1], (K,), -HMAX, HMAX + 1)
    third = jax.random.randint(keys[2], (K,), 1, LMAX + 1)
    signs = 2 * jax.random.randint(keys[3], (K,), 0, 2) - 1
    triples = jnp.stack([first, second, third * signs]).astype(jnp.int32)
    triples = triples.at[:, 0].set(jnp.array([HMAX, -HMAX, LMAX], jnp.int32))
    triples = triples.at[:, 1].set(jnp.array([-HMAX, HMAX, -LMAX], jnp.int32))
    return triples


def block_levels(rng, shape, cuts, least, top_value):
    level, own = 1.0, jax.random.fold_in(rng, 6)
    for dim, blocks in cuts:
        steps = jnp.exp(jax.random.uniform(jax.random.fold_in(own, dim), (blocks,), jnp.float32, least / len(cuts), top_value / len(cuts)))
        level = level * jnp.repeat(steps, shape[dim] // blocks).reshape([-1 if axis == dim else 1 for axis in range(len(shape))])
    return level


def setup_inputs(seed: int = 0, part: int = 0) -> dict:
    key_list = jax.random.split(jax.random.key(seed), 7)
    own_keys = jax.random.split(jax.random.fold_in(key_list[6], part), 7)
    return {
        "coords": jnp.clip(1.0 * jax.random.uniform(own_keys[0], (3, ION_SLOT_TOTAL), jnp.float32) ** block_levels(own_keys[0], (3, ION_SLOT_TOTAL), ((1, 16),), -0.2, 0.2), 0.0, 1.0),
        "charges": jnp.clip(jax.random.uniform(own_keys[1], (ION_SLOT_TOTAL,), jnp.float32, -1.0, 1.0) * block_levels(own_keys[1], (ION_SLOT_TOTAL,), ((0, 16),), -0.4, 0.0), -1.0, 1.0),
        "counts": draw_counts(jax.random.fold_in(jax.random.fold_in(key_list[6], part), 71), part),
        "send_slot": draw_send_slot(jax.random.fold_in(jax.random.fold_in(key_list[6], part), 71), part),
        "recv_index": draw_recv_index(jax.random.fold_in(jax.random.fold_in(key_list[6], part), 71), part),
        "wave_ints": draw_wave_ints(jax.random.fold_in(key_list[6], 71), part),
    }


DOUBLE_PI = 2.0 * math.pi
EWALD_BETA = 30.0
BOX_Z = 3.0
FORCE_GAIN = 400.0

def phys_vectors(wave_float):
    return jnp.stack([DOUBLE_PI * wave_float[0], DOUBLE_PI * wave_float[1], DOUBLE_PI * wave_float[2] / BOX_Z])

def phase_angles(wave_float, frac):
    inner = wave_float[0][:, None] * frac[0][None, :] + wave_float[1][:, None] * frac[1][None, :]
    inner = inner + wave_float[2][:, None] * frac[2][None, :]
    return DOUBLE_PI * inner

def pull_sum(wave_float, cos_weighted, sin_weighted, frac):
    angles = phase_angles(wave_float, frac)
    coef = jnp.sin(angles) * cos_weighted[:, None] - jnp.cos(angles) * sin_weighted[:, None]
    wave_phys = phys_vectors(wave_float)
    return lax.optimization_barrier(jnp.sum(wave_phys[:, :, None] * coef[None, :, :], axis=1))

def reference(coords, charges, counts, send_slot, recv_index, wave_ints):
    devices = counts.shape[0]
    slots_dev = charges.shape[0] // devices
    atoms_dev = recv_index.shape[0] // devices
    pair_cap = 2 * atoms_dev // devices
    buf_width = devices * pair_cap
    slot_ids = jnp.arange(slots_dev, dtype=jnp.int32)
    is_live = slot_ids[None, :] < counts[:, None]
    source = jnp.arange(devices, dtype=jnp.int32)[:, None]
    target_slot = jnp.where(is_live, source * buf_width + send_slot.reshape(devices, slots_dev), devices * buf_width)
    target_slot = target_slot.reshape(-1).astype(jnp.int32)
    value_entries = jnp.concatenate([coords, charges[None, :]], axis=0)
    table = jnp.zeros((4, devices * buf_width), jnp.float32).at[:, target_slot].set(value_entries, mode='drop')
    dest = jnp.repeat(jnp.arange(devices, dtype=jnp.int32), atoms_dev)
    where_from = (recv_index // pair_cap * buf_width + dest * pair_cap + recv_index % pair_cap).astype(jnp.int32)
    atom_rows = table[:, where_from]
    n_total = atom_rows.shape[1]
    wave_float = wave_ints.astype(jnp.float32)
    k_block = 128
    k_blocks = wave_float.reshape(3, K // k_block, k_block).transpose(1, 0, 2)

    def block_sums(wave_part):
        angles = phase_angles(wave_part, atom_rows[:3])
        return (lax.optimization_barrier(jnp.sum(atom_rows[3][None, :] * jnp.cos(angles), axis=1)), lax.optimization_barrier(jnp.sum(atom_rows[3][None, :] * jnp.sin(angles), axis=1)))
    cos_sum, sin_sum = lax.map(block_sums, k_blocks)
    cos_sum = cos_sum.reshape(-1)
    sin_sum = sin_sum.reshape(-1)
    wave_phys = phys_vectors(wave_float)
    k_squared = lax.optimization_barrier(jnp.sum(wave_phys * wave_phys, axis=0))
    weight = jnp.exp(-k_squared / (4.0 * EWALD_BETA * EWALD_BETA)) / k_squared
    cos_weighted = weight * cos_sum
    sin_weighted = weight * sin_sum
    force_scale = FORCE_GAIN / math.sqrt(float(n_total * K))
    a_block = 1024
    atom_blocks = atom_rows.reshape(4, n_total // a_block, a_block).transpose(1, 0, 2)

    def force_of_block(block_rows):
        pull_total = pull_sum(wave_float, cos_weighted, sin_weighted, block_rows[:3])
        return force_scale * block_rows[3][None, :] * pull_total
    atom_forces = lax.map(force_of_block, atom_blocks).transpose(1, 0, 2).reshape(3, n_total)
    back = jnp.zeros((3, devices * buf_width), jnp.float32).at[:, where_from].set(atom_forces)
    picked = back[:, jnp.minimum(target_slot, devices * buf_width - 1)]
    slot_forces = jnp.where(is_live.reshape(-1)[None, :], picked, 0.0)
    return (slot_forces, atom_forces)
```

```python
import functools
import math

import jax
import jax.numpy as jnp
from jax import lax
from jax.experimental import pallas as pl
from jax.experimental.pallas import tpu as pltpu
from jax.sharding import PartitionSpec as P

EWALD_BETA = 30.0
BOX_Z = 3.0
FORCE_GAIN = 400.0
HMAX = 12
LMAX = 36
SIDE = 2 * HMAX
FOLD = (2 * HMAX + 1) * SIDE
PAIRS = 640
L_ROWS = 2 * LMAX
L_TILES = L_ROWS // 8
P_TILES = PAIRS // 128
TILES = L_TILES * P_TILES
F32 = jnp.float32
BF16 = jnp.bfloat16

SIN_C = [(-1) ** n * math.pi ** (2 * n + 1) / math.factorial(2 * n + 1) for n in range(7)]
COS_C = [(-1) ** n * math.pi ** (2 * n) / math.factorial(2 * n) for n in range(8)]
NT = (((1,), (1,)), ((), ()))
NN = (((1,), (0,)), ((), ()))


def iota(shape, dim):
    return lax.broadcasted_iota(jnp.int32, shape, dim)


def horner(coefs, u):
    out = jnp.full_like(u, coefs[-1])
    for c in coefs[-2::-1]:
        out = out * u + c
    return out


def turns(mult, frac):
    high = jnp.floor(frac * 4096.0 + 0.5) * (1.0 / 4096.0)
    low = frac - high
    whole = mult * high
    r = (whole - jnp.floor(whole + 0.5)) + mult * low
    u = r * r
    s = r * horner(SIN_C, u)
    c = horner(COS_C, u)
    return 1.0 - 2.0 * s * s, 2.0 * s * c


def split2(x):
    hi = x.astype(BF16)
    return hi, (x - hi.astype(F32)).astype(BF16)


def split3(x):
    hi = x.astype(BF16)
    rest = x - hi.astype(F32)
    mid = rest.astype(BF16)
    return hi, mid, (rest - mid.astype(F32)).astype(BF16)


def mm(a, b, dims):
    return lax.dot_general(a, b, dims, preferred_element_type=F32)


def l_column():
    row = iota((L_ROWS, 1), 0)
    return (4 * (row // 8) + row % 4 + 1).astype(F32), (row % 8) < 4


def pair_rows():
    n = iota((1, PAIRS), 1)
    tall = n < FOLD
    q = n // SIDE
    h = jnp.where(tall, q - HMAX, n - FOLD - HMAX)
    k = jnp.where(tall, n - q * SIDE - HMAX, HMAX)
    return h.astype(F32), k.astype(F32)


def fill_pairs(frac_x, frac_y, tables):
    width = frac_x.shape[1]
    mult = (iota((32, 1), 0) - HMAX).astype(F32)
    cx, sx = turns(mult, frac_x)
    cy, sy = turns(mult, frac_y)
    cyk, syk = cy[:SIDE], sy[:SIDE]

    def put(start, c, s):
        rows = pl.ds(start, c.shape[0])
        for value, (hi_ref, lo_ref) in ((c, tables[:2]), (s, tables[2:])):
            hi, lo = split2(value)
            hi_ref[rows, :] = hi
            lo_ref[rows, :] = lo

    def one(i):
        a, b = cx[i : i + 1], sx[i : i + 1]
        return a * cyk - b * syk, b * cyk + a * syk

    for i in range(0, 2 * HMAX, 2):
        (c0, s0), (c1, s1) = one(i), one(i + 1)
        put(i * SIDE, jnp.concatenate([c0, c1]), jnp.concatenate([s0, s1]))
    c0, s0 = one(2 * HMAX)
    a, b = cy[SIDE : SIDE + 1], sy[SIDE : SIDE + 1]
    pad = jnp.zeros((8, width), F32)
    put(
        2 * HMAX * SIDE,
        jnp.concatenate([c0, cx * a - sx * b, pad]),
        jnp.concatenate([s0, sx * a + cx * b, pad]),
    )


def tiles_out(ref, value, count):
    for t in range(count):
        if t < TILES:
            i, j = t // P_TILES, t % P_TILES
            ref[t] = value[8 * i : 8 * i + 8, 128 * j : 128 * j + 128]
        else:
            ref[t] = jnp.zeros((8, 128), F32)


def local_kernel(
    devices, rows, cap, tile_count,
    coords, charges, counts, send_slot, wave,
    sums, mult, posts, *tables,
):
    slots = coords.shape[1]
    me = lax.axis_index("blk") * rows + lax.axis_index("row")
    live = iota((1, slots), 1) < counts[...]
    q = jnp.where(live, charges[...], 0.0)
    target = jnp.where(live, send_slot[...], -1)
    width = devices * cap
    spots = jnp.where(target == iota((width, slots), 0), 1.0, 0.0).astype(BF16)
    entries = jnp.concatenate([coords[...], q, jnp.zeros((4, slots), F32)])
    out = sum(mm(term, spots, NT) for term in split3(entries))
    per_tile = 128 // cap
    lane_part = iota((8, 128), 1) // cap
    for d in range(devices):
        tile = out[:, 128 * (d // per_tile) : 128 * (d // per_tile) + 128]
        tile = jnp.where(lane_part == d % per_tile, tile, 0.0)
        shift = (me % per_tile - d % per_tile + per_tile) % per_tile * cap
        posts[d] = pltpu.roll(tile, shift, 1)
    k_local = wave.shape[1]
    part = k_local // rows
    split = part % 128 == 0 and part * rows == k_local
    if split:
        w = wave[:, pl.ds(pl.multiple_of(lax.axis_index("row") * part, 128), part)]
    else:
        w = wave[...]
    h, k, l = w[0:1], w[1:2], w[2:3]
    sign = jnp.where(l < 0, -1, 1)
    h, k, l = h * sign, k * sign, l * sign
    if not split:
        l = jnp.where(lax.axis_index("row") == 0, l, 0)
    n = jnp.where(k < HMAX, (h + HMAX) * SIDE + k + HMAX, FOLD + HMAX + h)
    l_col, is_re = l_column()
    of_l = jnp.where(l.astype(F32) == l_col, 1.0, 0.0).astype(BF16)
    of_pair = jnp.where(n == iota((PAIRS, n.shape[1]), 0), 1.0, 0.0).astype(BF16)
    times = mm(of_l, of_pair, NT)
    hf, kf = pair_rows()
    two_pi = 2.0 * math.pi
    px, py, pz = two_pi * hf, two_pi * kf, two_pi * l_col / BOX_Z
    k2 = px * px + py * py + pz * pz
    weight = jnp.exp(-k2 / (4.0 * EWALD_BETA * EWALD_BETA)) / k2
    tiles_out(mult, times * weight, tile_count)
    fill_pairs(coords[0:1], coords[1:2], tables)
    cz, sz = turns(l_col, coords[2:3])
    v1h, v1l = split2(q * jnp.where(is_re, cz, sz))
    v2h, v2l = split2(q * jnp.where(is_re, -sz, cz))
    uch, ucl, ush, usl = (t[...] for t in tables)
    total = mm(v1l, uch, NT) + mm(v1h, ucl, NT) + mm(v2l, ush, NT) + mm(v2h, usl, NT)
    total = total + (mm(v1h, uch, NT) + mm(v2h, ush, NT))
    tiles_out(sums, total, tile_count)


def exchange_kernel(
    devices, rows, cap,
    sums, mult, posts,
    grid, atoms,
    got_m, got_p, got_t, own, m_s, m_r, p_s, p_r, t_s, t_r, g_s, g_r,
):
    me = lax.axis_index("blk") * rows + lax.axis_index("row")
    share = sums.shape[0] // devices
    per_tile = 128 // cap

    def to(o):
        d = (me + o) % devices
        return d, {"blk": d // rows, "row": d % rows}

    barrier = pltpu.get_barrier_semaphore()

    @pl.loop(1, devices)
    def _(o):
        pl.semaphore_signal(
            barrier, inc=1, device_id=to(o)[1], device_id_type=pl.DeviceIdType.MESH
        )

    pl.semaphore_wait(barrier, devices - 1)

    def copy(src, dst, s, r, o, dev):
        return pltpu.make_async_remote_copy(
            src_ref=src, dst_ref=dst, send_sem=s.at[o], recv_sem=r.at[o],
            device_id=dev, device_id_type=pl.DeviceIdType.MESH,
        )

    def mult_copy(o):
        d, dev = to(o)
        return copy(mult.at[pl.ds(d * share, share)], got_m.at[o], m_s, m_r, o, dev)

    def post_copy(o):
        d, dev = to(o)
        return copy(posts.at[d], got_p.at[o], p_s, p_r, o, dev)

    def sums_copy(o):
        d, dev = to(o)
        return copy(sums.at[pl.ds(d * share, share)], got_t.at[o], t_s, t_r, o, dev)

    def grid_copy(o):
        _, dev = to(o)
        return copy(own, grid.at[pl.ds(me * share, share)], g_s, g_r, o, dev)

    def each(f):
        @pl.loop(1, devices)
        def _(o):
            f(o)

    each(lambda o: sums_copy(o).start())
    each(lambda o: mult_copy(o).start())
    each(lambda o: post_copy(o).start())
    got_t[0] = sums[pl.ds(me * share, share)]
    got_m[0] = mult[pl.ds(me * share, share)]
    got_p[0] = posts[me]
    each(lambda o: sums_copy(o).wait_recv())
    each(lambda o: mult_copy(o).wait_recv())
    piece = jnp.sum(got_t[...], axis=0) * jnp.sum(got_m[...], axis=0)
    own[...] = piece
    each(lambda o: grid_copy(o).start())
    grid[pl.ds(me * share, share)] = piece
    each(lambda o: post_copy(o).wait_recv())
    for t in range(atoms.shape[0]):
        tile = jnp.zeros((8, 128), F32)
        for s in range(t * per_tile, min((t + 1) * per_tile, devices)):
            tile = tile + got_p[(me - s + devices) % devices]
        atoms[t] = tile
    each(lambda o: grid_copy(o).wait_recv())
    each(lambda o: sums_copy(o).wait_send())
    each(lambda o: mult_copy(o).wait_send())
    each(lambda o: post_copy(o).wait_send())
    each(lambda o: grid_copy(o).wait_send())


def force_kernel(
    scale,
    coords, charges, counts, recv_index, grid, arrived,
    slot_forces, atom_forces,
    *tables,
):
    slots = coords.shape[1]
    atoms = recv_index.shape[1]
    live = iota((1, slots), 1) < counts[...]
    q = jnp.where(live, charges[...], 0.0)
    table = jnp.concatenate([arrived[t] for t in range(arrived.shape[0])], axis=1)
    index = recv_index[...]
    picks = jnp.where(index == iota((table.shape[1], atoms), 0), 1.0, 0.0).astype(BF16)
    rows = sum(mm(term, picks, NN) for term in split3(table))
    frac = [jnp.concatenate([coords[i : i + 1], rows[i : i + 1]], axis=1) for i in range(3)]
    charge = jnp.concatenate([q, rows[3:4]], axis=1)
    fill_pairs(frac[0], frac[1], tables)
    l_col, is_re = l_column()
    cz, sz = turns(l_col, frac[2])
    vf = jnp.where(is_re, sz, cz)
    hf, kf = pair_rows()
    tile = lambda i, j: grid[i * P_TILES + j]
    g = jnp.concatenate(
        [jnp.concatenate([tile(i, j) for j in range(P_TILES)], axis=1) for i in range(L_TILES)]
    )
    swap = jnp.concatenate(
        [
            part
            for i in range(L_TILES)
            for part in (g[8 * i + 4 : 8 * i + 8], g[8 * i : 8 * i + 4])
        ]
    )
    gc = jnp.where(is_re, g, -g)
    gch, gcl = split2(jnp.concatenate([gc, gc * hf, gc * kf]))
    gsh, gsl = split2(jnp.concatenate([swap, swap * hf, swap * kf]))
    uch, ucl, ush, usl = (t[...] for t in tables)
    x = mm(gcl, uch, NN) + mm(gch, ucl, NN) + mm(gsl, ush, NN) + mm(gsh, usl, NN)
    x = x + (mm(gch, uch, NN) + mm(gsh, ush, NN))
    x = x * jnp.concatenate([vf] * 3)
    two_pi = 2.0 * math.pi
    fz = jnp.sum(x[:L_ROWS] * (two_pi * l_col / BOX_Z), axis=0, keepdims=True)
    fx = two_pi * jnp.sum(x[L_ROWS : 2 * L_ROWS], axis=0, keepdims=True)
    fy = two_pi * jnp.sum(x[2 * L_ROWS :], axis=0, keepdims=True)
    force = scale * charge * jnp.concatenate([fx, fy, fz])
    slot_forces[...] = jnp.where(live, force[:, :slots], 0.0)
    atom_forces[...] = force[:, slots:]


VMEM = pl.BlockSpec(memory_space=pltpu.VMEM)


def body(coords, charges, counts, send_slot, recv_index, wave_ints):
    slots = charges.shape[0]
    atoms_dev = recv_index.shape[0]
    blks, rows = lax.axis_size("blk"), lax.axis_size("row")
    devices = blks * rows
    cap = 2 * atoms_dev // devices
    share = -(-TILES // devices)
    tile_count = share * devices
    arrivals = devices * cap // 128
    scale = FORCE_GAIN / math.sqrt(float(atoms_dev * devices * blks * wave_ints.shape[1]))
    q, count = charges[None, :], counts[:, None]
    shape = jax.ShapeDtypeStruct
    big = pltpu.CompilerParams(vmem_limit_bytes=56 * 2**20)
    sums, mult, posts = pl.pallas_call(
        functools.partial(local_kernel, devices, rows, cap, tile_count),
        out_shape=[
            shape((tile_count, 8, 128), F32),
            shape((tile_count, 8, 128), F32),
            shape((devices, 8, 128), F32),
        ],
        in_specs=[VMEM] * 5,
        out_specs=[VMEM] * 3,
        scratch_shapes=[pltpu.VMEM((PAIRS, slots), BF16)] * 4,
        compiler_params=big,
    )(coords, q, count, send_slot[None, :], wave_ints)
    dma = pltpu.SemaphoreType.DMA((devices,))
    grid, arrived = pl.pallas_call(
        functools.partial(exchange_kernel, devices, rows, cap),
        out_shape=[shape((tile_count, 8, 128), F32), shape((arrivals, 8, 128), F32)],
        in_specs=[VMEM] * 3,
        out_specs=[VMEM] * 2,
        scratch_shapes=[
            pltpu.VMEM((devices, share, 8, 128), F32),
            pltpu.VMEM((devices, 8, 128), F32),
            pltpu.VMEM((devices, share, 8, 128), F32),
            pltpu.VMEM((share, 8, 128), F32),
        ]
        + [dma] * 8,
        compiler_params=pltpu.CompilerParams(
            collective_id=0, has_side_effects=True, vmem_limit_bytes=56 * 2**20
        ),
    )(sums, mult, posts)
    return pl.pallas_call(
        functools.partial(force_kernel, scale),
        out_shape=[shape((3, slots), F32), shape((3, atoms_dev), F32)],
        in_specs=[VMEM] * 6,
        out_specs=[VMEM] * 2,
        scratch_shapes=[pltpu.VMEM((PAIRS, slots + atoms_dev), BF16)] * 4,
        compiler_params=big,
    )(coords, q, count, recv_index[None, :], grid, arrived)


def solution(mesh):
    ions = P(("groups", "blk", "row"))
    return jax.shard_map(
        body,
        mesh=mesh,
        in_specs=(P(None, *ions), ions, ions, ions, ions, P(None, "blk")),
        out_specs=(P(None, *ions), P(None, *ions)),
        check_vma=False,
    )
```

```python
import functools
import math

import jax
import jax.numpy as jnp
from jax import lax
from jax.experimental import pallas as pl
from jax.experimental.pallas import tpu as pltpu
from jax.sharding import PartitionSpec as P

EWALD_BETA = 30.0
BOX_Z = 3.0
FORCE_GAIN = 400.0
HMAX = 12
LMAX = 36
SIDE = 2 * HMAX
FOLD = (2 * HMAX + 1) * SIDE
PAIRS = 640
L_ROWS = 2 * LMAX
L_TILES = L_ROWS // 8
P_TILES = PAIRS // 128
TILES = L_TILES * P_TILES
F32 = jnp.float32
BF16 = jnp.bfloat16

SIN_C = [(-1) ** n * math.pi ** (2 * n + 1) / math.factorial(2 * n + 1) for n in range(7)]
COS_C = [(-1) ** n * math.pi ** (2 * n) / math.factorial(2 * n) for n in range(8)]
NT = (((1,), (1,)), ((), ()))
NN = (((1,), (0,)), ((), ()))


def iota(shape, dim):
    return lax.broadcasted_iota(jnp.int32, shape, dim)


def horner(coefs, u):
    out = jnp.full_like(u, coefs[-1])
    for c in coefs[-2::-1]:
        out = out * u + c
    return out


def turns(mult, frac):
    high = jnp.floor(frac * 4096.0 + 0.5) * (1.0 / 4096.0)
    low = frac - high
    whole = mult * high
    r = (whole - jnp.floor(whole + 0.5)) + mult * low
    u = r * r
    s = r * horner(SIN_C, u)
    c = horner(COS_C, u)
    return 1.0 - 2.0 * s * s, 2.0 * s * c


def split2(x):
    hi = x.astype(BF16)
    return hi, (x - hi.astype(F32)).astype(BF16)


def split3(x):
    hi = x.astype(BF16)
    rest = x - hi.astype(F32)
    mid = rest.astype(BF16)
    return hi, mid, (rest - mid.astype(F32)).astype(BF16)


def mm(a, b, dims):
    return lax.dot_general(a, b, dims, preferred_element_type=F32)


def l_column():
    row = iota((L_ROWS, 1), 0)
    return (4 * (row // 8) + row % 4 + 1).astype(F32), (row % 8) < 4


def pair_rows():
    n = iota((1, PAIRS), 1)
    tall = n < FOLD
    q = n // SIDE
    h = jnp.where(tall, q - HMAX, n - FOLD - HMAX)
    k = jnp.where(tall, n - q * SIDE - HMAX, HMAX)
    return h.astype(F32), k.astype(F32)


def fill_pairs(frac_x, frac_y, tables, first):
    width = frac_x.shape[1]
    lanes = pl.ds(first, width)
    mult = (iota((32, 1), 0) - HMAX).astype(F32)
    cx, sx = turns(mult, frac_x)
    cy, sy = turns(mult, frac_y)
    cyk, syk = cy[:SIDE], sy[:SIDE]

    def put(start, c, s):
        rows = pl.ds(start, c.shape[0])
        for value, (hi_ref, lo_ref) in ((c, tables[:2]), (s, tables[2:])):
            hi, lo = split2(value)
            hi_ref[rows, lanes] = hi
            lo_ref[rows, lanes] = lo

    def one(i):
        a, b = cx[i : i + 1], sx[i : i + 1]
        return a * cyk - b * syk, b * cyk + a * syk

    for i in range(0, 2 * HMAX, 2):
        (c0, s0), (c1, s1) = one(i), one(i + 1)
        put(i * SIDE, jnp.concatenate([c0, c1]), jnp.concatenate([s0, s1]))
    c0, s0 = one(2 * HMAX)
    a, b = cy[SIDE : SIDE + 1], sy[SIDE : SIDE + 1]
    pad = jnp.zeros((8, width), F32)
    put(
        2 * HMAX * SIDE,
        jnp.concatenate([c0, cx * a - sx * b, pad]),
        jnp.concatenate([s0, sx * a + cx * b, pad]),
    )


def tiles_out(ref, value, count):
    for t in range(count):
        if t < TILES:
            i, j = t // P_TILES, t % P_TILES
            ref[t] = value[8 * i : 8 * i + 8, 128 * j : 128 * j + 128]
        else:
            ref[t] = jnp.zeros((8, 128), F32)


def each(count, f):
    if count <= 16:
        for o in range(1, count):
            f(o)
    else:
        pl.loop(1, count)(f)


def kernel(
    blks, rows, cap, scale,
    coords, charges, counts, send_slot, recv_index, wave,
    slot_forces, atom_forces,
    uch_ref, ucl_ref, ush_ref, usl_ref, mail, got_mail, sums, from_sib, half_sums, got_t, own, grid,
    m_s, m_r, x_s, x_r, t_s, t_r, g_s, g_r, f_s, f_r,
):
    devices = blks * rows
    chips = devices // 2
    slots = coords.shape[1]
    atoms = recv_index.shape[0]
    blk, row = lax.axis_index("blk"), lax.axis_index("row")
    me = blk * rows + row
    core = blk % 2
    chip = blk // 2 * rows + row
    share = own.shape[0]
    half = chips * share
    tile_count = 2 * half
    mine = core * half
    tables = (uch_ref, ucl_ref, ush_ref, usl_ref)
    mesh_id = pl.DeviceIdType.MESH
    sibling = {"blk": blk + 1 - 2 * core, "row": row}

    def other(o):
        d = (me + o) % devices
        return d, {"blk": d // rows, "row": d % rows}

    def other_chip(o):
        c = (chip + o) % chips
        return c, {"blk": c // rows * 2 + core, "row": c % rows}

    def copy(src, dst, s, r, o, dev):
        return pltpu.make_async_remote_copy(
            src_ref=src, dst_ref=dst, send_sem=s.at[o], recv_sem=r.at[o],
            device_id=dev, device_id_type=mesh_id,
        )

    def mail_copy(o):
        d, dev = other(o)
        return copy(mail.at[d], got_mail.at[o], m_s, m_r, o, dev)

    def sib_copy():
        return copy(sums.at[pl.ds(half - mine, half)], from_sib, x_s, x_r, 0, sibling)

    def sums_copy(o):
        c, dev = other_chip(o)
        return copy(half_sums.at[pl.ds(c * share, share)], got_t.at[o], t_s, t_r, o, dev)

    def grid_copy(o):
        _, dev = other_chip(o)
        return copy(own, grid.at[pl.ds(mine + chip * share, share)], g_s, g_r, o, dev)

    def pass_on(o):
        c = (chip + chips - o) % chips
        place = grid.at[pl.ds(mine + c * share, share)]
        return copy(own if isinstance(o, int) and o == 0 else place, place, f_s, f_r, o, sibling)

    barrier = pltpu.get_barrier_semaphore()
    each(
        devices,
        lambda o: pl.semaphore_signal(
            barrier, inc=1, device_id=other(o)[1], device_id_type=mesh_id
        ),
    )

    live = iota((1, slots), 1) < counts[0]
    q = jnp.where(live, charges[...].reshape(1, slots), 0.0)
    target = jnp.where(live, send_slot[...].reshape(1, slots), -1)
    spots = jnp.where(target == iota((devices * cap, slots), 0), 1.0, 0.0).astype(BF16)
    entries = jnp.concatenate([coords[...], q, jnp.zeros((4, slots), F32)])
    out = sum(mm(term, spots, NT) for term in split3(entries))
    per_tile = 128 // cap
    lane_part = iota((8, 128), 1) // cap
    for d in range(devices):
        tile = out[:, 128 * (d // per_tile) : 128 * (d // per_tile) + 128]
        tile = jnp.where(lane_part == d % per_tile, tile, 0.0)
        shift = (me % per_tile - d % per_tile + per_tile) % per_tile * cap
        mail[d, share] = pltpu.roll(tile, shift, 1)[:4]
    k_local = wave.shape[1]
    part = k_local // rows
    split = part % 128 == 0 and part * rows == k_local
    w = wave[:, pl.ds(pl.multiple_of(row * part, 128), part)] if split else wave[...]
    h, k, l = w[0:1], w[1:2], w[2:3]
    sign = jnp.where(l < 0, -1, 1)
    h, k, l = h * sign, k * sign, l * sign
    if not split:
        l = jnp.where(row == 0, l, 0)
    n = jnp.where(k < HMAX, (h + HMAX) * SIDE + k + HMAX, FOLD + HMAX + h)
    l_col, is_re = l_column()
    of_l = jnp.where(l.astype(F32) == l_col, 1.0, 0.0).astype(BF16)
    of_pair = jnp.where(n == iota((PAIRS, n.shape[1]), 0), 1.0, 0.0).astype(BF16)
    times = mm(of_l, of_pair, NT)
    hf, kf = pair_rows()
    two_pi = 2.0 * math.pi
    px, py, pz = two_pi * hf, two_pi * kf, two_pi * l_col / BOX_Z
    k2 = px * px + py * py + pz * pz
    times = times * (jnp.exp(-k2 / (4.0 * EWALD_BETA * EWALD_BETA)) / k2)
    for t in range(tile_count):
        c, piece = t // half, t % half // share
        d = (piece // rows * 2 + c) * rows + piece % rows
        if t < TILES:
            i, j = t // P_TILES, t % P_TILES
            mail[d, t % share] = times[8 * i : 8 * i + 4, 128 * j : 128 * j + 128]
        else:
            mail[d, t % share] = jnp.zeros((4, 128), F32)
    pl.semaphore_wait(barrier, devices - 1)
    each(devices, lambda o: mail_copy(o).start())

    fill_pairs(coords[0:1], coords[1:2], tables, 0)
    cz, sz = turns(l_col, coords[2:3])
    v1h, v1l = split2(q * jnp.where(is_re, cz, sz))
    v2h, v2l = split2(q * jnp.where(is_re, -sz, cz))
    uch, ucl, ush, usl = (t[:, :slots] for t in tables)
    total = mm(v1l, uch, NT) + mm(v1h, ucl, NT) + mm(v2l, ush, NT) + mm(v2h, usl, NT)
    total = total + (mm(v1h, uch, NT) + mm(v2h, ush, NT))
    for t in range(tile_count):
        if t < TILES:
            i, j = t // P_TILES, t % P_TILES
            sums[t] = total[8 * i : 8 * i + 8, 128 * j : 128 * j + 128]
        else:
            sums[t] = jnp.zeros((8, 128), F32)
    sib_copy().start()

    each(devices, lambda o: mail_copy(o).wait_recv())
    got_mail[0] = mail[me]
    arrived = []
    for t in range(devices // per_tile):
        tile = jnp.zeros((4, 128), F32)
        for s in range(t * per_tile, (t + 1) * per_tile):
            tile = tile + got_mail[(me - s + devices) % devices, share]
        arrived.append(tile)
    table = jnp.concatenate(arrived, axis=1)
    table = jnp.concatenate([table, jnp.zeros_like(table)])
    index = recv_index[...].reshape(1, atoms)
    picks = jnp.where(index == iota((table.shape[1], atoms), 0), 1.0, 0.0).astype(BF16)
    ions = sum(mm(term, picks, NN) for term in split3(table))
    m_own = got_mail[0, :share]
    for o in range(1, devices):
        m_own = m_own + got_mail[o, :share]

    sib_copy().wait_recv()
    half_sums[...] = sums[pl.ds(mine, half)] + from_sib[...]
    each(chips, lambda o: sums_copy(o).start())
    fill_pairs(ions[0:1], ions[1:2], tables, slots)
    each(chips, lambda o: sums_copy(o).wait_recv())
    got_t[0] = half_sums[pl.ds(chip * share, share)]
    piece = jnp.sum(got_t[...], axis=0) * jnp.concatenate([m_own, m_own], axis=1)
    own[...] = piece
    each(chips, lambda o: grid_copy(o).start())
    pass_on(0).start()
    grid[pl.ds(mine + chip * share, share)] = piece
    cz2, sz2 = turns(l_col, ions[2:3])
    vf = jnp.where(is_re, jnp.concatenate([sz, sz2], axis=1), jnp.concatenate([cz, cz2], axis=1))
    charge = jnp.concatenate([q, ions[3:4]], axis=1)

    def forward(o):
        grid_copy(o).wait_recv()
        pass_on(o).start()

    each(chips, forward)
    pass_on(0).wait_recv()
    each(chips, lambda o: pass_on(o).wait_recv())

    tile = lambda i, j: grid[i * P_TILES + j]
    g = jnp.concatenate(
        [jnp.concatenate([tile(i, j) for j in range(P_TILES)], axis=1) for i in range(L_TILES)]
    )
    swap = jnp.concatenate(
        [
            rows4
            for i in range(L_TILES)
            for rows4 in (g[8 * i + 4 : 8 * i + 8], g[8 * i : 8 * i + 4])
        ]
    )
    gc = jnp.where(is_re, g, -g)
    gch, gcl = split2(jnp.concatenate([gc, gc * hf, gc * kf]))
    gsh, gsl = split2(jnp.concatenate([swap, swap * hf, swap * kf]))
    uch, ucl, ush, usl = (t[...] for t in tables)
    x = mm(gcl, uch, NN) + mm(gch, ucl, NN) + mm(gsl, ush, NN) + mm(gsh, usl, NN)
    x = x + (mm(gch, uch, NN) + mm(gsh, ush, NN))
    x = x * jnp.concatenate([vf] * 3)
    fz = jnp.sum(x[:L_ROWS] * (two_pi * l_col / BOX_Z), axis=0, keepdims=True)
    fx = two_pi * jnp.sum(x[L_ROWS : 2 * L_ROWS], axis=0, keepdims=True)
    fy = two_pi * jnp.sum(x[2 * L_ROWS :], axis=0, keepdims=True)
    force = scale * charge * jnp.concatenate([fx, fy, fz])
    slot_forces[...] = jnp.where(live, force[:, :slots], 0.0)
    atom_forces[...] = force[:, slots:]

    each(devices, lambda o: mail_copy(o).wait_send())
    sib_copy().wait_send()
    each(chips, lambda o: sums_copy(o).wait_send())
    each(chips, lambda o: grid_copy(o).wait_send())
    pass_on(0).wait_send()
    each(chips, lambda o: pass_on(o).wait_send())


VMEM = pl.BlockSpec(memory_space=pltpu.VMEM)
SMEM = pl.BlockSpec(memory_space=pltpu.SMEM)


def body(coords, charges, counts, send_slot, recv_index, wave_ints):
    slots = charges.shape[0]
    atoms = recv_index.shape[0]
    blks, rows = lax.axis_size("blk"), lax.axis_size("row")
    devices = blks * rows
    chips = devices // 2
    cap = 2 * atoms // devices
    share = -(-TILES // devices)
    half = chips * share
    scale = FORCE_GAIN / math.sqrt(float(atoms * devices * blks * wave_ints.shape[1]))
    shape = jax.ShapeDtypeStruct
    dma = lambda n: [pltpu.SemaphoreType.DMA((n,))] * 2
    return pl.pallas_call(
        functools.partial(kernel, blks, rows, cap, scale),
        out_shape=[shape((3, slots), F32), shape((3, atoms), F32)],
        in_specs=[VMEM, VMEM, SMEM, VMEM, VMEM, VMEM],
        out_specs=[VMEM] * 2,
        scratch_shapes=[pltpu.VMEM((PAIRS, slots + atoms), BF16)] * 4
        + [
            pltpu.VMEM((devices, share + 1, 4, 128), F32),
            pltpu.VMEM((devices, share + 1, 4, 128), F32),
            pltpu.VMEM((2 * half, 8, 128), F32),
            pltpu.VMEM((half, 8, 128), F32),
            pltpu.VMEM((half, 8, 128), F32),
            pltpu.VMEM((chips, share, 8, 128), F32),
            pltpu.VMEM((share, 8, 128), F32),
            pltpu.VMEM((2 * half, 8, 128), F32),
        ]
        + dma(devices) + dma(1) + dma(chips) + dma(chips) + dma(chips),
        compiler_params=pltpu.CompilerParams(
            collective_id=0, has_side_effects=True, vmem_limit_bytes=56 * 2**20
        ),
    )(coords, charges, counts, send_slot, recv_index, wave_ints)


def solution(mesh):
    ions = P(("groups", "blk", "row"))
    return jax.shard_map(
        body,
        mesh=mesh,
        in_specs=(P(None, *ions), ions, ions, ions, ions, P(None, "blk")),
        out_specs=(P(None, *ions), P(None, *ions)),
        check_vma=False,
    )
```

```python
import functools
import math

import jax
import jax.numpy as jnp
from jax import lax
from jax.experimental import pallas as pl
from jax.experimental.pallas import tpu as pltpu
from jax.sharding import PartitionSpec as P

EWALD_BETA = 30.0
BOX_Z = 3.0
FORCE_GAIN = 400.0
HMAX = 12
LMAX = 36
SIDE = 2 * HMAX
FOLD = (2 * HMAX + 1) * SIDE
PAIRS = 640
L_ROWS = 2 * LMAX
L_TILES = L_ROWS // 8
P_TILES = PAIRS // 128
TILES = L_TILES * P_TILES
F32 = jnp.float32
BF16 = jnp.bfloat16

SIN_C = [(-1) ** n * math.pi ** (2 * n + 1) / math.factorial(2 * n + 1) for n in range(7)]
COS_C = [(-1) ** n * math.pi ** (2 * n) / math.factorial(2 * n) for n in range(8)]
NT = (((1,), (1,)), ((), ()))
NN = (((1,), (0,)), ((), ()))


def iota(shape, dim):
    return lax.broadcasted_iota(jnp.int32, shape, dim)


def horner(coefs, u):
    out = jnp.full_like(u, coefs[-1])
    for c in coefs[-2::-1]:
        out = out * u + c
    return out


def turns(mult, frac):
    high = jnp.floor(frac * 4096.0 + 0.5) * (1.0 / 4096.0)
    low = frac - high
    whole = mult * high
    r = (whole - jnp.floor(whole + 0.5)) + mult * low
    u = r * r
    s = r * horner(SIN_C, u)
    c = horner(COS_C, u)
    return 1.0 - 2.0 * s * s, 2.0 * s * c


def split2(x):
    hi = x.astype(BF16)
    return hi, (x - hi.astype(F32)).astype(BF16)


def split3(x):
    hi = x.astype(BF16)
    rest = x - hi.astype(F32)
    mid = rest.astype(BF16)
    return hi, mid, (rest - mid.astype(F32)).astype(BF16)


def mm(a, b, dims):
    return lax.dot_general(a, b, dims, preferred_element_type=F32)


def l_column():
    row = iota((L_ROWS, 1), 0)
    return (4 * (row // 8) + row % 4 + 1).astype(F32), (row % 8) < 4


def pair_rows():
    n = iota((1, PAIRS), 1)
    tall = n < FOLD
    q = n // SIDE
    h = jnp.where(tall, q - HMAX, n - FOLD - HMAX)
    k = jnp.where(tall, n - q * SIDE - HMAX, HMAX)
    return h.astype(F32), k.astype(F32)


def fill_pairs(frac_x, frac_y, table, first):
    width = frac_x.shape[1]
    lanes = pl.ds(first, width)
    mult = (iota((32, 1), 0) - HMAX).astype(F32)
    cx, sx = turns(mult, frac_x)
    cy, sy = turns(mult, frac_y)
    cyk, syk = cy[:SIDE], sy[:SIDE]

    def put(start, c, s):
        for part, value in enumerate((c, s)):
            hi, lo = split2(value)
            table[pl.ds(part * PAIRS + start, c.shape[0]), lanes] = hi
            table[pl.ds((part + 2) * PAIRS + start, c.shape[0]), lanes] = lo

    def one(i):
        a, b = cx[i : i + 1], sx[i : i + 1]
        return a * cyk - b * syk, b * cyk + a * syk

    for i in range(0, 2 * HMAX, 2):
        (c0, s0), (c1, s1) = one(i), one(i + 1)
        put(i * SIDE, jnp.concatenate([c0, c1]), jnp.concatenate([s0, s1]))
    c0, s0 = one(2 * HMAX)
    a, b = cy[SIDE : SIDE + 1], sy[SIDE : SIDE + 1]
    pad = jnp.zeros((8, width), F32)
    put(
        2 * HMAX * SIDE,
        jnp.concatenate([c0, cx * a - sx * b, pad]),
        jnp.concatenate([s0, sx * a + cx * b, pad]),
    )


def tiles_out(ref, value, count):
    for t in range(count):
        if t < TILES:
            i, j = t // P_TILES, t % P_TILES
            ref[t] = value[8 * i : 8 * i + 8, 128 * j : 128 * j + 128]
        else:
            ref[t] = jnp.zeros((8, 128), F32)


def each(count, f):
    if count <= 16:
        for o in range(1, count):
            f(o)
    else:
        pl.loop(1, count)(f)


def kernel(
    blks, rows, cap, scale,
    coords, charges, counts, send_slot, recv_index, wave,
    forces,
    table, mail, got_mail, sums, from_sib, half_sums, got_t, own, grid,
    m_s, m_r, x_s, x_r, t_s, t_r, g_s, g_r, f_s, f_r,
):
    devices = blks * rows
    chips = devices // 2
    slots = coords.shape[1]
    atoms = recv_index.shape[0]
    blk, row = lax.axis_index("blk"), lax.axis_index("row")
    me = blk * rows + row
    core = blk % 2
    chip = blk // 2 * rows + row
    share = own.shape[0]
    half = chips * share
    tile_count = 2 * half
    mine = core * half
    mesh_id = pl.DeviceIdType.MESH
    sibling = {"blk": blk + 1 - 2 * core, "row": row}

    def other(o):
        d = (me + o) % devices
        return d, {"blk": d // rows, "row": d % rows}

    def other_chip(o):
        c = (chip + o) % chips
        return c, {"blk": c // rows * 2 + core, "row": c % rows}

    def copy(src, dst, s, r, o, dev):
        return pltpu.make_async_remote_copy(
            src_ref=src, dst_ref=dst, send_sem=s.at[o], recv_sem=r.at[o],
            device_id=dev, device_id_type=mesh_id,
        )

    def mail_copy(o):
        d, dev = other(o)
        return copy(mail.at[d], got_mail.at[o], m_s, m_r, o, dev)

    def sib_copy():
        return copy(sums.at[pl.ds(half - mine, half)], from_sib, x_s, x_r, 0, sibling)

    def sums_copy(o):
        c, dev = other_chip(o)
        return copy(half_sums.at[pl.ds(c * share, share)], got_t.at[o], t_s, t_r, o, dev)

    def grid_copy(o):
        _, dev = other_chip(o)
        return copy(own, grid.at[pl.ds(mine + chip * share, share)], g_s, g_r, o, dev)

    def pass_on(o):
        c = (chip + chips - o) % chips
        place = grid.at[pl.ds(mine + c * share, share)]
        return copy(own if isinstance(o, int) and o == 0 else place, place, f_s, f_r, o, sibling)

    barrier = pltpu.get_barrier_semaphore()
    each(
        devices,
        lambda o: pl.semaphore_signal(
            barrier, inc=1, device_id=other(o)[1], device_id_type=mesh_id
        ),
    )

    live = iota((1, slots), 1) < counts[0]
    q = jnp.where(live, charges[...].reshape(1, slots), 0.0)
    target = jnp.where(live, send_slot[...].reshape(1, slots), -1)
    spots = jnp.where(target == iota((devices * cap, slots), 0), 1.0, 0.0).astype(BF16)
    entries = jnp.concatenate([coords[...], q, jnp.zeros((4, slots), F32)])
    out = sum(mm(term, spots, NT) for term in split3(entries))
    per_tile = 128 // cap
    lane_part = iota((8, 128), 1) // cap
    for d in range(devices):
        tile = out[:, 128 * (d // per_tile) : 128 * (d // per_tile) + 128]
        tile = jnp.where(lane_part == d % per_tile, tile, 0.0)
        shift = (me % per_tile - d % per_tile + per_tile) % per_tile * cap
        mail[d, share] = pltpu.roll(tile, shift, 1)[:4]
    k_local = wave.shape[1]
    part = k_local // rows
    split = part % 128 == 0 and part * rows == k_local
    w = wave[:, pl.ds(pl.multiple_of(row * part, 128), part)] if split else wave[...]
    h, k, l = w[0:1], w[1:2], w[2:3]
    sign = jnp.where(l < 0, -1, 1)
    h, k, l = h * sign, k * sign, l * sign
    if not split:
        l = jnp.where(row == 0, l, 0)
    n = jnp.where(k < HMAX, (h + HMAX) * SIDE + k + HMAX, FOLD + HMAX + h)
    l_col, is_re = l_column()
    of_l = jnp.where(l.astype(F32) == l_col, 1.0, 0.0).astype(BF16)
    of_pair = jnp.where(n == iota((PAIRS, n.shape[1]), 0), 1.0, 0.0).astype(BF16)
    times = mm(of_l, of_pair, NT)
    hf, kf = pair_rows()
    two_pi = 2.0 * math.pi
    px, py, pz = two_pi * hf, two_pi * kf, two_pi * l_col / BOX_Z
    k2 = px * px + py * py + pz * pz
    times = times * (jnp.exp(-k2 / (4.0 * EWALD_BETA * EWALD_BETA)) / k2)
    for t in range(tile_count):
        c, piece = t // half, t % half // share
        d = (piece // rows * 2 + c) * rows + piece % rows
        if t < TILES:
            i, j = t // P_TILES, t % P_TILES
            mail[d, t % share] = times[8 * i : 8 * i + 4, 128 * j : 128 * j + 128]
        else:
            mail[d, t % share] = jnp.zeros((4, 128), F32)

    fill_pairs(coords[0:1], coords[1:2], table, 0)
    pl.semaphore_wait(barrier, devices - 1)
    each(devices, lambda o: mail_copy(o).start())
    cz, sz = turns(l_col, coords[2:3])
    v1h, v1l = split2(q * jnp.where(is_re, cz, sz))
    v2h, v2l = split2(q * jnp.where(is_re, -sz, cz))
    uch, ush, ucl, usl = (table[pl.ds(i * PAIRS, PAIRS), :slots] for i in range(4))
    total = mm(v1l, uch, NT) + mm(v1h, ucl, NT) + mm(v2l, ush, NT) + mm(v2h, usl, NT)
    total = total + (mm(v1h, uch, NT) + mm(v2h, ush, NT))
    for t in range(tile_count):
        if t < TILES:
            i, j = t // P_TILES, t % P_TILES
            sums[t] = total[8 * i : 8 * i + 8, 128 * j : 128 * j + 128]
        else:
            sums[t] = jnp.zeros((8, 128), F32)
    sib_copy().start()
    sib_copy().wait_recv()
    half_sums[...] = sums[pl.ds(mine, half)] + from_sib[...]
    each(chips, lambda o: sums_copy(o).start())

    each(devices, lambda o: mail_copy(o).wait_recv())
    got_mail[0] = mail[me]
    arrived = []
    for t in range(devices // per_tile):
        tile = jnp.zeros((4, 128), F32)
        for s in range(t * per_tile, (t + 1) * per_tile):
            tile = tile + got_mail[(me - s + devices) % devices, share]
        arrived.append(tile)
    came = jnp.concatenate(arrived, axis=1)
    came = jnp.concatenate([came, jnp.zeros_like(came)])
    index = recv_index[...].reshape(1, atoms)
    picks = jnp.where(index == iota((came.shape[1], atoms), 0), 1.0, 0.0).astype(BF16)
    ions = sum(mm(term, picks, NN) for term in split3(came))
    m_own = got_mail[0, :share]
    for o in range(1, devices):
        m_own = m_own + got_mail[o, :share]

    fill_pairs(ions[0:1], ions[1:2], table, slots)
    each(chips, lambda o: sums_copy(o).wait_recv())
    got_t[0] = half_sums[pl.ds(chip * share, share)]
    piece = jnp.sum(got_t[...], axis=0) * jnp.concatenate([m_own, m_own], axis=1)
    own[...] = piece
    each(chips, lambda o: grid_copy(o).start())
    pass_on(0).start()
    grid[pl.ds(mine + chip * share, share)] = piece
    cz2, sz2 = turns(l_col, ions[2:3])
    vf = jnp.where(is_re, jnp.concatenate([sz, sz2], axis=1), jnp.concatenate([cz, cz2], axis=1))
    charge = jnp.concatenate([q, ions[3:4]], axis=1)

    def forward(o):
        grid_copy(o).wait_recv()
        pass_on(o).start()

    each(chips, forward)
    pass_on(0).wait_recv()
    each(chips, lambda o: pass_on(o).wait_recv())

    tile = lambda i, j: grid[i * P_TILES + j]
    g = jnp.concatenate(
        [jnp.concatenate([tile(i, j) for j in range(P_TILES)], axis=1) for i in range(L_TILES)]
    )
    swap = jnp.concatenate(
        [
            rows4
            for i in range(L_TILES)
            for rows4 in (g[8 * i + 4 : 8 * i + 8], g[8 * i : 8 * i + 4])
        ]
    )
    gc = jnp.where(is_re, g, -g)
    gch, gcl = split2(jnp.concatenate([gc, gc * hf, gc * kf]))
    gsh, gsl = split2(jnp.concatenate([swap, swap * hf, swap * kf]))
    x = mm(jnp.concatenate([gch, gsh] * 2, axis=1), table[...], NN)
    x = x + mm(jnp.concatenate([gcl, gsl], axis=1), table[: 2 * PAIRS], NN)
    x = x * jnp.concatenate([vf] * 3)
    fz = jnp.sum(x[:L_ROWS] * (two_pi * l_col / BOX_Z), axis=0, keepdims=True)
    fx = two_pi * jnp.sum(x[L_ROWS : 2 * L_ROWS], axis=0, keepdims=True)
    fy = two_pi * jnp.sum(x[2 * L_ROWS :], axis=0, keepdims=True)
    forces[...] = scale * charge * jnp.concatenate([fx, fy, fz])

    each(devices, lambda o: mail_copy(o).wait_send())
    sib_copy().wait_send()
    each(chips, lambda o: sums_copy(o).wait_send())
    each(chips, lambda o: grid_copy(o).wait_send())
    pass_on(0).wait_send()
    each(chips, lambda o: pass_on(o).wait_send())


def deliver(counts, forces, slot_forces, atom_forces):
    slots = slot_forces.shape[1]
    live = iota((1, slots), 1) < counts[0]
    slot_forces[...] = jnp.where(live, forces[:, :slots], 0.0)
    atom_forces[...] = forces[:, slots:]


VMEM = pl.BlockSpec(memory_space=pltpu.VMEM)
SMEM = pl.BlockSpec(memory_space=pltpu.SMEM)


def body(coords, charges, counts, send_slot, recv_index, wave_ints):
    slots = charges.shape[0]
    atoms = recv_index.shape[0]
    blks, rows = lax.axis_size("blk"), lax.axis_size("row")
    devices = blks * rows
    chips = devices // 2
    cap = 2 * atoms // devices
    share = -(-TILES // devices)
    half = chips * share
    scale = FORCE_GAIN / math.sqrt(float(atoms * devices * blks * wave_ints.shape[1]))
    shape = jax.ShapeDtypeStruct
    dma = lambda n: [pltpu.SemaphoreType.DMA((n,))] * 2
    forces = pl.pallas_call(
        functools.partial(kernel, blks, rows, cap, scale),
        out_shape=shape((3, slots + atoms), F32),
        in_specs=[VMEM, VMEM, SMEM, VMEM, VMEM, VMEM],
        out_specs=VMEM,
        scratch_shapes=[pltpu.VMEM((4 * PAIRS, slots + atoms), BF16)]
        + [
            pltpu.VMEM((devices, share + 1, 4, 128), F32),
            pltpu.VMEM((devices, share + 1, 4, 128), F32),
            pltpu.VMEM((2 * half, 8, 128), F32),
            pltpu.VMEM((half, 8, 128), F32),
            pltpu.VMEM((half, 8, 128), F32),
            pltpu.VMEM((chips, share, 8, 128), F32),
            pltpu.VMEM((share, 8, 128), F32),
            pltpu.VMEM((2 * half, 8, 128), F32),
        ]
        + dma(devices) + dma(1) + dma(chips) + dma(chips) + dma(chips),
        compiler_params=pltpu.CompilerParams(
            collective_id=0, has_side_effects=True, vmem_limit_bytes=56 * 2**20
        ),
    )(coords, charges, counts, send_slot, recv_index, wave_ints)
    return pl.pallas_call(
        deliver,
        out_shape=[shape((3, slots), F32), shape((3, atoms), F32)],
        in_specs=[SMEM, VMEM],
        out_specs=[VMEM] * 2,
    )(counts, forces)


def solution(mesh):
    ions = P(("groups", "blk", "row"))
    return jax.shard_map(
        body,
        mesh=mesh,
        in_specs=(P(None, *ions), ions, ions, ions, ions, P(None, "blk")),
        out_specs=(P(None, *ions), P(None, *ions)),
        check_vma=False,
    )
```

```python
import functools
import math

import jax
import jax.numpy as jnp
from jax import lax
from jax.experimental import pallas as pl
from jax.experimental.pallas import tpu as pltpu
from jax.sharding import PartitionSpec as P

EWALD_BETA = 30.0
BOX_Z = 3.0
FORCE_GAIN = 400.0
HMAX = 12
LMAX = 36
SIDE = 2 * HMAX
FOLD = (2 * HMAX + 1) * SIDE
PAIRS = 640
L_ROWS = 2 * LMAX
L_TILES = L_ROWS // 8
P_TILES = PAIRS // 128
TILES = L_TILES * P_TILES
F32 = jnp.float32
BF16 = jnp.bfloat16

SIN_C = [(-1) ** n * math.pi ** (2 * n + 1) / math.factorial(2 * n + 1) for n in range(7)]
COS_C = [(-1) ** n * math.pi ** (2 * n) / math.factorial(2 * n) for n in range(8)]
NT = (((1,), (1,)), ((), ()))
NN = (((1,), (0,)), ((), ()))


def iota(shape, dim):
    return lax.broadcasted_iota(jnp.int32, shape, dim)


def horner(coefs, u):
    out = jnp.full_like(u, coefs[-1])
    for c in coefs[-2::-1]:
        out = out * u + c
    return out


def turns(mult, frac):
    high = jnp.floor(frac * 4096.0 + 0.5) * (1.0 / 4096.0)
    low = frac - high
    whole = mult * high
    r = (whole - jnp.floor(whole + 0.5)) + mult * low
    u = r * r
    s = r * horner(SIN_C, u)
    c = horner(COS_C, u)
    return 1.0 - 2.0 * s * s, 2.0 * s * c


def split2(x):
    hi = x.astype(BF16)
    return hi, (x - hi.astype(F32)).astype(BF16)


def split3(x):
    hi = x.astype(BF16)
    rest = x - hi.astype(F32)
    mid = rest.astype(BF16)
    return hi, mid, (rest - mid.astype(F32)).astype(BF16)


def mm(a, b, dims):
    return lax.dot_general(a, b, dims, preferred_element_type=F32)


def l_column():
    row = iota((L_ROWS, 1), 0)
    return (4 * (row // 8) + row % 4 + 1).astype(F32), (row % 8) < 4


def pair_rows():
    n = iota((1, PAIRS), 1)
    tall = n < FOLD
    q = n // SIDE
    h = jnp.where(tall, q - HMAX, n - FOLD - HMAX)
    k = jnp.where(tall, n - q * SIDE - HMAX, HMAX)
    return h.astype(F32), k.astype(F32)


def fill_pairs(frac_x, frac_y, table, first):
    width = frac_x.shape[1]
    lanes = pl.ds(first, width)
    mult = (iota((32, 1), 0) - HMAX).astype(F32)
    cx, sx = turns(mult, frac_x)
    cy, sy = turns(mult, frac_y)
    cyk, syk = cy[:SIDE], sy[:SIDE]

    def put(start, c, s):
        for part, value in enumerate((c, s)):
            hi, lo = split2(value)
            table[pl.ds(part * PAIRS + start, c.shape[0]), lanes] = hi
            table[pl.ds((part + 2) * PAIRS + start, c.shape[0]), lanes] = lo

    def one(i):
        a, b = cx[i : i + 1], sx[i : i + 1]
        return a * cyk - b * syk, b * cyk + a * syk

    for i in range(0, 2 * HMAX, 2):
        (c0, s0), (c1, s1) = one(i), one(i + 1)
        put(i * SIDE, jnp.concatenate([c0, c1]), jnp.concatenate([s0, s1]))
    c0, s0 = one(2 * HMAX)
    a, b = cy[SIDE : SIDE + 1], sy[SIDE : SIDE + 1]
    pad = jnp.zeros((8, width), F32)
    put(
        2 * HMAX * SIDE,
        jnp.concatenate([c0, cx * a - sx * b, pad]),
        jnp.concatenate([s0, sx * a + cx * b, pad]),
    )


def tiles_out(ref, value, count):
    for t in range(count):
        if t < TILES:
            i, j = t // P_TILES, t % P_TILES
            ref[t] = value[8 * i : 8 * i + 8, 128 * j : 128 * j + 128]
        else:
            ref[t] = jnp.zeros((8, 128), F32)


def each(count, f):
    if count <= 16:
        for o in range(1, count):
            f(o)
    else:
        pl.loop(1, count)(f)


def kernel(
    blks, rows, cap, scale,
    coords, charges, counts, send_slot, recv_index, wave,
    forces,
    table, mail, got_mail, sums, from_sib, half_sums, got_t, own, grid,
    m_s, m_r, x_s, x_r, t_s, t_r, g_s, g_r, f_s, f_r,
):
    devices = blks * rows
    chips = devices // 2
    slots = coords.shape[1]
    atoms = recv_index.shape[0]
    blk, row = lax.axis_index("blk"), lax.axis_index("row")
    me = blk * rows + row
    core = blk % 2
    chip = blk // 2 * rows + row
    share = own.shape[0]
    half = chips * share
    tile_count = 2 * half
    mine = core * half
    mesh_id = pl.DeviceIdType.MESH
    sibling = {"blk": blk + 1 - 2 * core, "row": row}

    def other(o):
        d = (me + o) % devices
        return d, {"blk": d // rows, "row": d % rows}

    def other_chip(o):
        c = (chip + o) % chips
        return c, {"blk": c // rows * 2 + core, "row": c % rows}

    def copy(src, dst, s, r, o, dev):
        return pltpu.make_async_remote_copy(
            src_ref=src, dst_ref=dst, send_sem=s.at[o], recv_sem=r.at[o],
            device_id=dev, device_id_type=mesh_id,
        )

    def mail_copy(o):
        d, dev = other(o)
        return copy(mail.at[d], got_mail.at[o], m_s, m_r, o, dev)

    def sib_copy():
        return copy(sums.at[pl.ds(half - mine, half)], from_sib, x_s, x_r, 0, sibling)

    def sums_copy(o):
        c, dev = other_chip(o)
        return copy(half_sums.at[pl.ds(c * share, share)], got_t.at[o], t_s, t_r, o, dev)

    def grid_copy(o):
        _, dev = other_chip(o)
        return copy(own, grid.at[pl.ds(mine + chip * share, share)], g_s, g_r, o, dev)

    def pass_on(o):
        c = (chip + chips - o) % chips
        place = grid.at[pl.ds(mine + c * share, share)]
        return copy(own if isinstance(o, int) and o == 0 else place, place, f_s, f_r, o, sibling)

    barrier = pltpu.get_barrier_semaphore()
    each(
        devices,
        lambda o: pl.semaphore_signal(
            barrier, inc=1, device_id=other(o)[1], device_id_type=mesh_id
        ),
    )

    live = iota((1, slots), 1) < counts[0]
    q = jnp.where(live, charges[...].reshape(1, slots), 0.0)
    target = jnp.where(live, send_slot[...].reshape(1, slots), -1)
    spots = jnp.where(target == iota((devices * cap, slots), 0), 1.0, 0.0).astype(BF16)
    entries = jnp.concatenate([coords[...], q, jnp.zeros((4, slots), F32)])
    terms = [*split3(entries), jnp.zeros((128 - 24, slots), BF16)]
    out = mm(spots, jnp.concatenate(terms), NT).T
    out = out[:8] + out[8:16] + out[16:24]
    per_tile = 128 // cap
    lane_part = iota((8, 128), 1) // cap
    for d in range(devices):
        tile = out[:, 128 * (d // per_tile) : 128 * (d // per_tile) + 128]
        tile = jnp.where(lane_part == d % per_tile, tile, 0.0)
        shift = (me % per_tile - d % per_tile + per_tile) % per_tile * cap
        mail[d, share] = pltpu.roll(tile, shift, 1)[:4]
    k_local = wave.shape[1]
    part = k_local // rows
    split = part % 128 == 0 and part * rows == k_local
    w = wave[:, pl.ds(pl.multiple_of(row * part, 128), part)] if split else wave[...]
    h, k, l = w[0:1], w[1:2], w[2:3]
    sign = jnp.where(l < 0, -1, 1)
    h, k, l = h * sign, k * sign, l * sign
    if not split:
        l = jnp.where(row == 0, l, 0)
    n = jnp.where(k < HMAX, (h + HMAX) * SIDE + k + HMAX, FOLD + HMAX + h)
    l_col, is_re = l_column()
    of_l = jnp.where(l.astype(F32) == l_col, 1.0, 0.0).astype(BF16)
    of_pair = jnp.where(n == iota((PAIRS, n.shape[1]), 0), 1.0, 0.0).astype(BF16)
    of_l = jnp.concatenate([of_l, jnp.zeros((128 - L_ROWS, of_l.shape[1]), BF16)])
    times = mm(of_pair, of_l, NT).T[:L_ROWS]
    hf, kf = pair_rows()
    two_pi = 2.0 * math.pi
    px, py, pz = two_pi * hf, two_pi * kf, two_pi * l_col / BOX_Z
    k2 = px * px + py * py + pz * pz
    times = times * (jnp.exp(-k2 / (4.0 * EWALD_BETA * EWALD_BETA)) / k2)
    for t in range(tile_count):
        c, piece = t // half, t % half // share
        d = (piece // rows * 2 + c) * rows + piece % rows
        if t < TILES:
            i, j = t // P_TILES, t % P_TILES
            mail[d, t % share] = times[8 * i : 8 * i + 4, 128 * j : 128 * j + 128]
        else:
            mail[d, t % share] = jnp.zeros((4, 128), F32)

    fill_pairs(coords[0:1], coords[1:2], table, 0)
    pl.semaphore_wait(barrier, devices - 1)
    each(devices, lambda o: mail_copy(o).start())
    cz, sz = turns(l_col, coords[2:3])
    wide = 128
    blank = jnp.zeros((wide - L_ROWS, slots), F32)
    v1h, v1l = split2(jnp.concatenate([q * jnp.where(is_re, cz, sz), blank]))
    v2h, v2l = split2(jnp.concatenate([q * jnp.where(is_re, -sz, cz), blank]))
    uch, ush, ucl, usl = (table[pl.ds(i * PAIRS, PAIRS), :slots] for i in range(4))
    low = mm(ucl, v1h, NT) + mm(usl, v2h, NT)
    both = mm(uch, jnp.concatenate([v1h, v1l]), NT) + mm(ush, jnp.concatenate([v2h, v2l]), NT)
    total = (both[:, :wide] + (both[:, wide:] + low)).T
    for t in range(tile_count):
        if t < TILES:
            i, j = t // P_TILES, t % P_TILES
            sums[t] = total[8 * i : 8 * i + 8, 128 * j : 128 * j + 128]
        else:
            sums[t] = jnp.zeros((8, 128), F32)
    sib_copy().start()
    sib_copy().wait_recv()
    half_sums[...] = sums[pl.ds(mine, half)] + from_sib[...]
    each(chips, lambda o: sums_copy(o).start())

    each(devices, lambda o: mail_copy(o).wait_recv())
    got_mail[0] = mail[me]
    arrived = []
    for t in range(devices // per_tile):
        tile = jnp.zeros((4, 128), F32)
        for s in range(t * per_tile, (t + 1) * per_tile):
            tile = tile + got_mail[(me - s + devices) % devices, share]
        arrived.append(tile)
    came = jnp.concatenate(arrived, axis=1)
    came = jnp.concatenate([came, jnp.zeros_like(came)])
    index = recv_index[...].reshape(1, atoms)
    picks = jnp.where(index == iota((came.shape[1], atoms), 0), 1.0, 0.0).astype(BF16)
    ions = sum(mm(term, picks, NN) for term in split3(came))
    m_own = got_mail[0, :share]
    for o in range(1, devices):
        m_own = m_own + got_mail[o, :share]

    fill_pairs(ions[0:1], ions[1:2], table, slots)
    each(chips, lambda o: sums_copy(o).wait_recv())
    got_t[0] = half_sums[pl.ds(chip * share, share)]
    piece = jnp.sum(got_t[...], axis=0) * jnp.concatenate([m_own, m_own], axis=1)
    own[...] = piece
    each(chips, lambda o: grid_copy(o).start())
    pass_on(0).start()
    grid[pl.ds(mine + chip * share, share)] = piece
    cz2, sz2 = turns(l_col, ions[2:3])
    vf = jnp.where(is_re, jnp.concatenate([sz, sz2], axis=1), jnp.concatenate([cz, cz2], axis=1))
    charge = jnp.concatenate([q, ions[3:4]], axis=1)

    def forward(o):
        grid_copy(o).wait_recv()
        pass_on(o).start()

    each(chips, forward)
    pass_on(0).wait_recv()
    each(chips, lambda o: pass_on(o).wait_recv())

    tile = lambda i, j: grid[i * P_TILES + j]
    g = jnp.concatenate(
        [jnp.concatenate([tile(i, j) for j in range(P_TILES)], axis=1) for i in range(L_TILES)]
    )
    swap = jnp.concatenate(
        [
            rows4
            for i in range(L_TILES)
            for rows4 in (g[8 * i + 4 : 8 * i + 8], g[8 * i : 8 * i + 4])
        ]
    )
    gc = jnp.where(is_re, g, -g)
    gch, gcl = split2(jnp.concatenate([gc, gc * hf, gc * kf]))
    gsh, gsl = split2(jnp.concatenate([swap, swap * hf, swap * kf]))
    x = mm(jnp.concatenate([gch, gsh] * 2, axis=1), table[...], NN)
    x = x + mm(jnp.concatenate([gcl, gsl], axis=1), table[: 2 * PAIRS], NN)
    x = x * jnp.concatenate([vf] * 3)
    fz = jnp.sum(x[:L_ROWS] * (two_pi * l_col / BOX_Z), axis=0, keepdims=True)
    fx = two_pi * jnp.sum(x[L_ROWS : 2 * L_ROWS], axis=0, keepdims=True)
    fy = two_pi * jnp.sum(x[2 * L_ROWS :], axis=0, keepdims=True)
    force = scale * charge * jnp.concatenate([fx, fy, fz])
    forces[:, :slots] = jnp.where(live, force[:, :slots], 0.0)
    forces[:, slots:] = force[:, slots:]

    each(devices, lambda o: mail_copy(o).wait_send())
    sib_copy().wait_send()
    each(chips, lambda o: sums_copy(o).wait_send())
    each(chips, lambda o: grid_copy(o).wait_send())
    pass_on(0).wait_send()
    each(chips, lambda o: pass_on(o).wait_send())


def deliver(forces, slot_forces, atom_forces):
    slots = slot_forces.shape[1]
    slot_forces[...] = forces[:, :slots]
    atom_forces[...] = forces[:, slots:]


VMEM = pl.BlockSpec(memory_space=pltpu.VMEM)
SMEM = pl.BlockSpec(memory_space=pltpu.SMEM)


def body(coords, charges, counts, send_slot, recv_index, wave_ints):
    slots = charges.shape[0]
    atoms = recv_index.shape[0]
    blks, rows = lax.axis_size("blk"), lax.axis_size("row")
    devices = blks * rows
    chips = devices // 2
    cap = 2 * atoms // devices
    share = -(-TILES // devices)
    half = chips * share
    scale = FORCE_GAIN / math.sqrt(float(atoms * devices * blks * wave_ints.shape[1]))
    shape = jax.ShapeDtypeStruct
    dma = lambda n: [pltpu.SemaphoreType.DMA((n,))] * 2
    forces = pl.pallas_call(
        functools.partial(kernel, blks, rows, cap, scale),
        out_shape=shape((3, slots + atoms), F32),
        in_specs=[VMEM, VMEM, SMEM, VMEM, VMEM, VMEM],
        out_specs=VMEM,
        scratch_shapes=[pltpu.VMEM((4 * PAIRS, slots + atoms), BF16)]
        + [
            pltpu.VMEM((devices, share + 1, 4, 128), F32),
            pltpu.VMEM((devices, share + 1, 4, 128), F32),
            pltpu.VMEM((2 * half, 8, 128), F32),
            pltpu.VMEM((half, 8, 128), F32),
            pltpu.VMEM((half, 8, 128), F32),
            pltpu.VMEM((chips, share, 8, 128), F32),
            pltpu.VMEM((share, 8, 128), F32),
            pltpu.VMEM((2 * half, 8, 128), F32),
        ]
        + dma(devices) + dma(1) + dma(chips) + dma(chips) + dma(chips),
        compiler_params=pltpu.CompilerParams(
            collective_id=0, has_side_effects=True, vmem_limit_bytes=56 * 2**20
        ),
    )(coords, charges, counts, send_slot, recv_index, wave_ints)
    return pl.pallas_call(
        deliver,
        out_shape=[shape((3, slots), F32), shape((3, atoms), F32)],
        in_specs=[VMEM],
        out_specs=[VMEM] * 2,
    )(forces)


def solution(mesh):
    ions = P(("groups", "blk", "row"))
    return jax.shard_map(
        body,
        mesh=mesh,
        in_specs=(P(None, *ions), ions, ions, ions, ions, P(None, "blk")),
        out_specs=(P(None, *ions), P(None, *ions)),
        check_vma=False,
    )
```

```python
import functools
import math

import jax
import jax.numpy as jnp
from jax import lax
from jax.experimental import pallas as pl
from jax.experimental.pallas import tpu as pltpu
from jax.sharding import PartitionSpec as P

EWALD_BETA = 30.0
BOX_Z = 3.0
FORCE_GAIN = 400.0
HMAX = 12
LMAX = 36
SIDE = 2 * HMAX
FOLD = (2 * HMAX + 1) * SIDE
PAIRS = 640
L_ROWS = 2 * LMAX
L_TILES = L_ROWS // 8
P_TILES = PAIRS // 128
TILES = L_TILES * P_TILES
F32 = jnp.float32
BF16 = jnp.bfloat16

SIN_C = [(-1) ** n * math.pi ** (2 * n + 1) / math.factorial(2 * n + 1) for n in range(7)]
COS_C = [(-1) ** n * math.pi ** (2 * n) / math.factorial(2 * n) for n in range(8)]
NT = (((1,), (1,)), ((), ()))
NN = (((1,), (0,)), ((), ()))


def iota(shape, dim):
    return lax.broadcasted_iota(jnp.int32, shape, dim)


def horner(coefs, u):
    out = jnp.full_like(u, coefs[-1])
    for c in coefs[-2::-1]:
        out = out * u + c
    return out


def turns(mult, frac):
    high = jnp.floor(frac * 4096.0 + 0.5) * (1.0 / 4096.0)
    low = frac - high
    whole = mult * high
    r = (whole - jnp.floor(whole + 0.5)) + mult * low
    u = r * r
    s = r * horner(SIN_C, u)
    c = horner(COS_C, u)
    return 1.0 - 2.0 * s * s, 2.0 * s * c


def split2(x):
    hi = x.astype(BF16)
    return hi, (x - hi.astype(F32)).astype(BF16)


def split3(x):
    hi = x.astype(BF16)
    rest = x - hi.astype(F32)
    mid = rest.astype(BF16)
    return hi, mid, (rest - mid.astype(F32)).astype(BF16)


def mm(a, b, dims):
    return lax.dot_general(a, b, dims, preferred_element_type=F32)


def l_column():
    row = iota((L_ROWS, 1), 0)
    return (4 * (row // 8) + row % 4 + 1).astype(F32), (row % 8) < 4


def pair_rows():
    n = iota((1, PAIRS), 1)
    tall = n < FOLD
    q = n // SIDE
    h = jnp.where(tall, q - HMAX, n - FOLD - HMAX)
    k = jnp.where(tall, n - q * SIDE - HMAX, HMAX)
    return h.astype(F32), k.astype(F32)


def fill_pairs(frac_x, frac_y, table, first):
    width = frac_x.shape[1]
    lanes = pl.ds(first, width)
    mult = (iota((32, 1), 0) - HMAX).astype(F32)
    cx, sx = turns(mult, frac_x)
    cy, sy = turns(mult, frac_y)
    cyk, syk = cy[:SIDE], sy[:SIDE]

    def put(start, c, s):
        for part, value in enumerate((c, s)):
            hi, lo = split2(value)
            table[pl.ds(part * PAIRS + start, c.shape[0]), lanes] = hi
            table[pl.ds((part + 2) * PAIRS + start, c.shape[0]), lanes] = lo

    def one(i):
        a, b = cx[i : i + 1], sx[i : i + 1]
        return a * cyk - b * syk, b * cyk + a * syk

    for i in range(0, 2 * HMAX, 2):
        (c0, s0), (c1, s1) = one(i), one(i + 1)
        put(i * SIDE, jnp.concatenate([c0, c1]), jnp.concatenate([s0, s1]))
    c0, s0 = one(2 * HMAX)
    a, b = cy[SIDE : SIDE + 1], sy[SIDE : SIDE + 1]
    pad = jnp.zeros((8, width), F32)
    put(
        2 * HMAX * SIDE,
        jnp.concatenate([c0, cx * a - sx * b, pad]),
        jnp.concatenate([s0, sx * a + cx * b, pad]),
    )


def tiles_out(ref, value, count):
    for t in range(count):
        if t < TILES:
            i, j = t // P_TILES, t % P_TILES
            ref[t] = value[8 * i : 8 * i + 8, 128 * j : 128 * j + 128]
        else:
            ref[t] = jnp.zeros((8, 128), F32)


def each(count, f):
    if count <= 16:
        for o in range(1, count):
            f(o)
    else:
        pl.loop(1, count)(f)


def kernel(
    blks, rows, cap, scale,
    coords, charges, counts, send_slot, recv_index, wave,
    forces,
    table, mail, got_mail, sums, from_sib, half_sums, got_t, own, grid,
    m_s, m_r, x_s, x_r, t_s, t_r, g_s, g_r, f_s, f_r,
):
    devices = blks * rows
    chips = devices // 2
    slots = coords.shape[1]
    atoms = recv_index.shape[0]
    blk, row = lax.axis_index("blk"), lax.axis_index("row")
    me = blk * rows + row
    core = blk % 2
    chip = blk // 2 * rows + row
    share = own.shape[0]
    half = chips * share
    tile_count = 2 * half
    mine = core * half
    mesh_id = pl.DeviceIdType.MESH
    sibling = {"blk": blk + 1 - 2 * core, "row": row}

    def other(o):
        d = (me + o) % devices
        return d, {"blk": d // rows, "row": d % rows}

    def other_chip(o):
        c = (chip + o) % chips
        return c, {"blk": c // rows * 2 + core, "row": c % rows}

    def copy(src, dst, s, r, o, dev):
        return pltpu.make_async_remote_copy(
            src_ref=src, dst_ref=dst, send_sem=s.at[o], recv_sem=r.at[o],
            device_id=dev, device_id_type=mesh_id,
        )

    def mail_copy(o):
        d, dev = other(o)
        return copy(mail.at[d], got_mail.at[o], m_s, m_r, o, dev)

    def sib_copy():
        return copy(sums.at[pl.ds(half - mine, half)], from_sib, x_s, x_r, 0, sibling)

    def sums_copy(o):
        c, dev = other_chip(o)
        return copy(half_sums.at[pl.ds(c * share, share)], got_t.at[o], t_s, t_r, o, dev)

    def grid_copy(o):
        _, dev = other_chip(o)
        return copy(own, grid.at[pl.ds(mine + chip * share, share)], g_s, g_r, o, dev)

    def pass_on(o):
        c = (chip + chips - o) % chips
        place = grid.at[pl.ds(mine + c * share, share)]
        return copy(own if isinstance(o, int) and o == 0 else place, place, f_s, f_r, o, sibling)

    barrier = pltpu.get_barrier_semaphore()
    each(
        devices,
        lambda o: pl.semaphore_signal(
            barrier, inc=1, device_id=other(o)[1], device_id_type=mesh_id
        ),
    )

    live = iota((1, slots), 1) < counts[0]
    q = jnp.where(live, charges[...].reshape(1, slots), 0.0)
    target = jnp.where(live, send_slot[...].reshape(1, slots), -1)
    spots = jnp.where(target == iota((devices * cap, slots), 0), 1.0, 0.0).astype(BF16)
    entries = jnp.concatenate([coords[...], q, jnp.zeros((4, slots), F32)])
    terms = [*split3(entries), jnp.zeros((128 - 24, slots), BF16)]
    out = mm(spots, jnp.concatenate(terms), NT).T
    out = out[:8] + out[8:16] + out[16:24]
    per_tile = 128 // cap
    lane_part = iota((8, 128), 1) // cap
    for d in range(devices):
        tile = out[:, 128 * (d // per_tile) : 128 * (d // per_tile) + 128]
        tile = jnp.where(lane_part == d % per_tile, tile, 0.0)
        shift = (me % per_tile - d % per_tile + per_tile) % per_tile * cap
        mail[d, share] = pltpu.roll(tile, shift, 1)[:4]
    k_local = wave.shape[1]
    part = k_local // rows
    split = part % 128 == 0 and part * rows == k_local
    w = wave[:, pl.ds(pl.multiple_of(row * part, 128), part)] if split else wave[...]
    h, k, l = w[0:1], w[1:2], w[2:3]
    sign = jnp.where(l < 0, -1, 1)
    h, k, l = h * sign, k * sign, l * sign
    if not split:
        l = jnp.where(row == 0, l, 0)
    n = jnp.where(k < HMAX, (h + HMAX) * SIDE + k + HMAX, FOLD + HMAX + h)
    l_col, is_re = l_column()
    of_l = jnp.where(l.astype(F32) == l_col, 1.0, 0.0).astype(BF16)
    of_pair = jnp.where(n == iota((PAIRS, n.shape[1]), 0), 1.0, 0.0).astype(BF16)
    of_l = jnp.concatenate([of_l, jnp.zeros((128 - L_ROWS, of_l.shape[1]), BF16)])
    times = mm(of_pair, of_l, NT).T[:L_ROWS]
    hf, kf = pair_rows()
    two_pi = 2.0 * math.pi
    px, py, pz = two_pi * hf, two_pi * kf, two_pi * l_col / BOX_Z
    k2 = px * px + py * py + pz * pz
    times = times * (jnp.exp(-k2 / (4.0 * EWALD_BETA * EWALD_BETA)) / k2)
    for t in range(tile_count):
        c, piece = t // half, t % half // share
        d = (piece // rows * 2 + c) * rows + piece % rows
        if t < TILES:
            i, j = t // P_TILES, t % P_TILES
            mail[d, t % share] = times[8 * i : 8 * i + 4, 128 * j : 128 * j + 128]
        else:
            mail[d, t % share] = jnp.zeros((4, 128), F32)

    fill_pairs(coords[0:1], coords[1:2], table, 0)
    pl.semaphore_wait(barrier, devices - 1)
    each(devices, lambda o: mail_copy(o).start())
    cz, sz = turns(l_col, coords[2:3])
    wide = 128
    blank = jnp.zeros((wide - L_ROWS, slots), F32)
    v1h, v1l = split2(jnp.concatenate([q * jnp.where(is_re, cz, sz), blank]))
    v2h, v2l = split2(jnp.concatenate([q * jnp.where(is_re, -sz, cz), blank]))
    uch, ush, ucl, usl = (table[pl.ds(i * PAIRS, PAIRS), :slots] for i in range(4))
    low = mm(ucl, v1h, NT) + mm(usl, v2h, NT)
    both = mm(uch, jnp.concatenate([v1h, v1l]), NT) + mm(ush, jnp.concatenate([v2h, v2l]), NT)
    total = (both[:, :wide] + (both[:, wide:] + low)).T
    for t in range(tile_count):
        if t < TILES:
            i, j = t // P_TILES, t % P_TILES
            sums[t] = total[8 * i : 8 * i + 8, 128 * j : 128 * j + 128]
        else:
            sums[t] = jnp.zeros((8, 128), F32)
    sib_copy().start()
    sib_copy().wait_recv()
    half_sums[...] = sums[pl.ds(mine, half)] + from_sib[...]
    each(chips, lambda o: sums_copy(o).start())

    each(devices, lambda o: mail_copy(o).wait_recv())
    got_mail[0] = mail[me]
    m_own = got_mail[0, :share]
    for o in range(1, devices):
        m_own = m_own + got_mail[o, :share]
    each(chips, lambda o: sums_copy(o).wait_recv())
    got_t[0] = half_sums[pl.ds(chip * share, share)]
    piece = jnp.sum(got_t[...], axis=0) * jnp.concatenate([m_own, m_own], axis=1)
    own[...] = piece
    each(chips, lambda o: grid_copy(o).start())
    pass_on(0).start()
    grid[pl.ds(mine + chip * share, share)] = piece
    arrived = []
    for t in range(devices // per_tile):
        tile = jnp.zeros((4, 128), F32)
        for s in range(t * per_tile, (t + 1) * per_tile):
            tile = tile + got_mail[(me - s + devices) % devices, share]
        arrived.append(tile)
    came = jnp.concatenate(arrived, axis=1)
    came = jnp.concatenate([came, jnp.zeros_like(came)])
    index = recv_index[...].reshape(1, atoms)
    picks = jnp.where(index == iota((came.shape[1], atoms), 0), 1.0, 0.0).astype(BF16)
    ions = sum(mm(term, picks, NN) for term in split3(came))
    fill_pairs(ions[0:1], ions[1:2], table, slots)
    cz2, sz2 = turns(l_col, ions[2:3])
    vf = jnp.where(is_re, jnp.concatenate([sz, sz2], axis=1), jnp.concatenate([cz, cz2], axis=1))
    charge = jnp.concatenate([q, ions[3:4]], axis=1)

    def forward(o):
        grid_copy(o).wait_recv()
        pass_on(o).start()

    each(chips, forward)
    pass_on(0).wait_recv()
    each(chips, lambda o: pass_on(o).wait_recv())

    tile = lambda i, j: grid[i * P_TILES + j]
    g = jnp.concatenate(
        [jnp.concatenate([tile(i, j) for j in range(P_TILES)], axis=1) for i in range(L_TILES)]
    )
    swap = jnp.concatenate(
        [
            rows4
            for i in range(L_TILES)
            for rows4 in (g[8 * i + 4 : 8 * i + 8], g[8 * i : 8 * i + 4])
        ]
    )
    gc = jnp.where(is_re, g, -g)
    gch, gcl = split2(jnp.concatenate([gc, gc * hf, gc * kf]))
    gsh, gsl = split2(jnp.concatenate([swap, swap * hf, swap * kf]))
    x = mm(jnp.concatenate([gch, gsh] * 2, axis=1), table[...], NN)
    x = x + mm(jnp.concatenate([gcl, gsl], axis=1), table[: 2 * PAIRS], NN)
    x = x * jnp.concatenate([vf] * 3)
    fz = jnp.sum(x[:L_ROWS] * (two_pi * l_col / BOX_Z), axis=0, keepdims=True)
    fx = two_pi * jnp.sum(x[L_ROWS : 2 * L_ROWS], axis=0, keepdims=True)
    fy = two_pi * jnp.sum(x[2 * L_ROWS :], axis=0, keepdims=True)
    force = scale * charge * jnp.concatenate([fx, fy, fz])
    forces[:, :slots] = jnp.where(live, force[:, :slots], 0.0)
    forces[:, slots:] = force[:, slots:]

    each(devices, lambda o: mail_copy(o).wait_send())
    sib_copy().wait_send()
    each(chips, lambda o: sums_copy(o).wait_send())
    each(chips, lambda o: grid_copy(o).wait_send())
    pass_on(0).wait_send()
    each(chips, lambda o: pass_on(o).wait_send())


def deliver(forces, slot_forces, atom_forces):
    slots = slot_forces.shape[1]
    slot_forces[...] = forces[:, :slots]
    atom_forces[...] = forces[:, slots:]


VMEM = pl.BlockSpec(memory_space=pltpu.VMEM)
SMEM = pl.BlockSpec(memory_space=pltpu.SMEM)


def body(coords, charges, counts, send_slot, recv_index, wave_ints):
    slots = charges.shape[0]
    atoms = recv_index.shape[0]
    blks, rows = lax.axis_size("blk"), lax.axis_size("row")
    devices = blks * rows
    chips = devices // 2
    cap = 2 * atoms // devices
    share = -(-TILES // devices)
    half = chips * share
    scale = FORCE_GAIN / math.sqrt(float(atoms * devices * blks * wave_ints.shape[1]))
    shape = jax.ShapeDtypeStruct
    dma = lambda n: [pltpu.SemaphoreType.DMA((n,))] * 2
    forces = pl.pallas_call(
        functools.partial(kernel, blks, rows, cap, scale),
        out_shape=shape((3, slots + atoms), F32),
        in_specs=[VMEM, VMEM, SMEM, VMEM, VMEM, VMEM],
        out_specs=VMEM,
        scratch_shapes=[pltpu.VMEM((4 * PAIRS, slots + atoms), BF16)]
        + [
            pltpu.VMEM((devices, share + 1, 4, 128), F32),
            pltpu.VMEM((devices, share + 1, 4, 128), F32),
            pltpu.VMEM((2 * half, 8, 128), F32),
            pltpu.VMEM((half, 8, 128), F32),
            pltpu.VMEM((half, 8, 128), F32),
            pltpu.VMEM((chips, share, 8, 128), F32),
            pltpu.VMEM((share, 8, 128), F32),
            pltpu.VMEM((2 * half, 8, 128), F32),
        ]
        + dma(devices) + dma(1) + dma(chips) + dma(chips) + dma(chips),
        compiler_params=pltpu.CompilerParams(
            collective_id=0, has_side_effects=True, vmem_limit_bytes=56 * 2**20
        ),
    )(coords, charges, counts, send_slot, recv_index, wave_ints)
    return pl.pallas_call(
        deliver,
        out_shape=[shape((3, slots), F32), shape((3, atoms), F32)],
        in_specs=[VMEM],
        out_specs=[VMEM] * 2,
    )(forces)


def solution(mesh):
    ions = P(("groups", "blk", "row"))
    return jax.shard_map(
        body,
        mesh=mesh,
        in_specs=(P(None, *ions), ions, ions, ions, ions, P(None, "blk")),
        out_specs=(P(None, *ions), P(None, *ions)),
        check_vma=False,
    )
```
